32 devices in a mesh: expert: 4 (over x, core), hidden: 8 (over z, y).
Axes of the slice: x: 2, y: 2, z: 4, core: 2. Of those that a mesh axis runs over, the one named last changes fastest.
Arguments:
- hidden_in: bfloat16 [512, 6144], P(('expert', 'hidden')), may hold values from -6 to 6
- norm_gain: float32 [6144], replicated, may hold values from 0.25 to 1.75
- router_weight: bfloat16 [6144, 4], replicated, may hold values from -0.078125 to 0.078125
- expert_ids: int32 [512, 2], P(('expert', 'hidden')), may hold values from 0 to 3, all different within a row; in each aligned block of 16 rows (0 to 15, 16 to 31, ...) at most 12 rows name the same one
- gate_proj: bfloat16 [4, 6144, 8192], P('expert', None, 'hidden'), may hold values from -0.078125 to 0.078125
- up_proj: bfloat16 [4, 6144, 8192], P('expert', None, 'hidden'), may hold values from -0.078125 to 0.078125
- down_proj: bfloat16 [4, 8192, 6144], P('expert', 'hidden'), may hold values from -0.0625 to 0.0625
Outputs:
- layer_out: bfloat16 [512, 6144], P(('expert', 'hidden'))
The draws below stay inside these ranges and needn't reach their ends.
Inputs may be any that keep to these rules, and one draw needn't show every extreme that they name: `expert_ids`: the two experts of a token differ. Within the rows of one device (aligned blocks of 16 tokens) no expert is named by more than 12 rows, a bound that some block reaches.
All inputs are finite; a program needn't handle non-finite values.
Results may differ from the reference program's by a relative error of at most 0.0085.
Values may be sent and summed in bfloat16 or wider, within the bound.
A program may use at most 128 MiB of HBM per device.

```python
import math
import jax
import jax.numpy as jnp
import numpy as np
from jax import lax

D = 6144
FF = 8192
TOP = 2
TOK_DEV = 16
EXPERTS = 4
CAP = 12
TOKENS = 512
N_EXPERT = 4
N_HIDDEN = 8


def block_scale(rng, extent, cuts, least, high):
    level, own = 1.0, jax.random.fold_in(rng, 6)
    for dim, shards_of in cuts:
        steps = jnp.exp(jax.random.uniform(jax.random.fold_in(own, dim), (shards_of,), jnp.float32, least / len(cuts), high / len(cuts)))
        level = level * jnp.repeat(steps, extent[dim] // shards_of).reshape([-1 if axis == dim else 1 for axis in range(len(extent))])
    return level


def routed_block(stream_key, own, number, rows, number_of, top, most, lean):
    sequence = jax.random.permutation(stream_key, number_of)
    crowded, common = load_shares(number_of, rows * top, most, lean, True), load_shares(number_of, rows * top, most, lean, False)
    places = jnp.arange(number_of)

    def named(tallies, rotation):
        used = int((tallies > 0).sum())
        fixed = max(1, used // 4)
        moved = fixed + (places - fixed + rotation * (used - fixed)) % max(1, number_of - fixed)
        return jnp.zeros((number_of,), jnp.int32).at[sequence[jnp.where(places < fixed, places, moved)]].set(jnp.asarray(tallies, jnp.int32))

    tallies = jnp.where(number % 4 == 0, named(crowded, number // 4), named(common, number - number // 4 - 1))
    mixed = jax.random.permutation(jax.random.fold_in(own, 3), number_of)
    source_of, sink = mixed[0:number_of // 2 * 2:2], mixed[1:number_of // 2 * 2:2]
    margin = jnp.minimum(tallies[source_of] - 1, most - tallies[sink]) // 2
    margin = jnp.where((source_of == sequence[0]) | (sink == sequence[0]) | (tallies[sink] == 0), 0, jnp.maximum(margin, 0))
    moved = jax.random.randint(jax.random.fold_in(own, 4), (number_of // 2,), 0, 1 << 20) % (margin + 1)
    tallies = tallies.at[source_of].add(-moved).at[sink].add(moved)
    members = jnp.searchsorted(jnp.cumsum(tallies), jnp.arange(rows * top), side="right").astype(jnp.int32)
    table = members.reshape(top, rows).T
    table = table[jax.random.permutation(jax.random.fold_in(own, 1), rows)]
    rotation = jax.random.randint(jax.random.fold_in(own, 2), (rows, 1), 0, top)
    return jnp.take_along_axis(table, (jnp.arange(top)[None, :] + rotation) % top, axis=1)


def load_shares(amount, total, limit, lean, full):
    loads = [(1 << 20) // math.isqrt(grade ** lean) + 1 for grade in range(1, amount + 1)]
    largest = limit if full else min(limit, max(-(-total // amount), total * loads[0] // sum(loads)))
    least = 1 if total - largest >= amount - 1 else 0
    given, surplus = [largest] + [least] * (amount - 1), total - largest - least * (amount - 1)
    while surplus > 0:
        free = [i for i in range(1, amount) if given[i] < largest] or [i for i in range(1, amount) if given[i] < limit]
        whole, remaining = sum([loads[i] for i in free]), surplus
        for i in free:
            more = min(limit - given[i], max(1, remaining * loads[i] // whole), surplus)
            given[i] = given[i] + more
            surplus = surplus - more
    return np.array(given)


def noise(rng, shape, deviation, limit, pieces=(), held_as=jnp.bfloat16):
    result = deviation * jax.random.normal(rng, shape, jnp.float32)
    if pieces:
        result = result * block_scale(rng, shape, pieces, -0.22, 0.18)
    return jnp.clip(result, -limit, limit).astype(held_as)


def setup_inputs(seed: int = 0) -> dict:
    streams_of = jax.random.split(jax.random.key(seed), 8)
    hidden_in = noise(streams_of[0], (TOKENS, D), 1.0, 6.0, ((0, 32),))
    norm_gain = jnp.clip(1.0 + 0.15 * jax.random.normal(streams_of[1], (D,), jnp.float32), 0.25, 1.75)
    router_weight = noise(streams_of[2], (D, EXPERTS), D ** -0.5, 0.078125)
    expert_ids_keys = jax.random.split(jax.random.fold_in(streams_of[3], 1), TOKENS // TOK_DEV)
    expert_ids_turns = jax.random.permutation(jax.random.fold_in(streams_of[3], 3), TOKENS // TOK_DEV)
    expert_ids = jax.vmap(lambda own, number: routed_block(jax.random.fold_in(streams_of[3], 2), own, number, TOK_DEV, EXPERTS, TOP, CAP, 2))(expert_ids_keys, expert_ids_turns).reshape((TOKENS, TOP))
    gate_proj = noise(streams_of[4], (EXPERTS, D, FF), D ** -0.5, 0.078125, ((0, 4), (2, 8)))
    up_proj = noise(streams_of[5], (EXPERTS, D, FF), D ** -0.5, 0.078125, ((0, 4), (2, 8)))
    down_proj = noise(streams_of[6], (EXPERTS, FF, D), FF ** -0.5, 0.0625, ((0, 4), (1, 8)))
    return dict(hidden_in=hidden_in, norm_gain=norm_gain, router_weight=router_weight, expert_ids=expert_ids, gate_proj=gate_proj, up_proj=up_proj, down_proj=down_proj)


def normalize(hidden_in, norm_gain):
    values = hidden_in.astype(jnp.float32)
    factor = lax.rsqrt(lax.optimization_barrier(jnp.mean(values * values, axis=-1, keepdims=True)) + 1e-05)
    return (values * factor * norm_gain).astype(jnp.bfloat16)

def gate_weights(normed, router_weight, expert_ids, experts):
    logits = jnp.dot(normed, router_weight, preferred_element_type=jnp.float32)
    picks = expert_ids[:, :, None] == jnp.arange(experts, dtype=jnp.int32)[None, None, :]
    chosen = lax.optimization_barrier(jnp.sum(jnp.where(picks, logits[:, None, :], 0.0), axis=-1))
    first = jax.nn.sigmoid(chosen[:, 0] - chosen[:, 1])
    return jnp.stack([first, 1.0 - first], axis=1)

def route_slots(block_ids, experts, capacity):
    flat_ids = block_ids.reshape(-1)
    onehot = (flat_ids[:, None] == jnp.arange(experts, dtype=jnp.int32)[None, :]).astype(jnp.int32)
    before = jnp.cumsum(onehot, axis=0) - onehot
    rank_in = lax.optimization_barrier(jnp.sum(before * onehot, axis=1))
    slot_place = (flat_ids * capacity + rank_in).astype(jnp.int32)
    owners = (jnp.arange(flat_ids.shape[0], dtype=jnp.int32) // block_ids.shape[1]).astype(jnp.int32)
    slot_token = jnp.zeros((experts * capacity,), jnp.int32).at[slot_place].set(owners)
    filled = jnp.zeros((experts * capacity,), jnp.bfloat16).at[slot_place].set(1.0)
    return (slot_place, slot_token, filled)

def expert_rows(rows, gate_w, up_w, down_w):
    gate = jnp.dot(rows, gate_w, preferred_element_type=jnp.float32)
    upper = jnp.dot(rows, up_w, preferred_element_type=jnp.float32)
    inner = (jax.nn.silu(gate) * upper).astype(jnp.bfloat16)
    block_width = FF // N_HIDDEN

    def add_block(total, index):
        start = index * block_width
        piece_h = lax.dynamic_slice_in_dim(inner, start, block_width, 1)
        piece_w = lax.dynamic_slice_in_dim(down_w, start, block_width, 0)
        term = jnp.dot(piece_h, piece_w, preferred_element_type=jnp.float32).astype(jnp.bfloat16)
        term = lax.optimization_barrier(term)
        return (total + term.astype(jnp.float32), None)
    total, _ = lax.scan(add_block, jnp.zeros((rows.shape[0], D), jnp.float32), jnp.arange(N_HIDDEN, dtype=jnp.int32))
    return total.astype(jnp.bfloat16)

def fill_block(normed_block, slot_token, filled):
    return jnp.take(normed_block, slot_token, axis=0) * filled[:, None]

def pick_block(returned_block, slot_place):
    return jnp.take(returned_block, slot_place, axis=0)

def route_block(block_ids):
    return route_slots(block_ids, EXPERTS, CAP)

def run_expert(packed):
    return expert_rows(packed[0], packed[1], packed[2], packed[3])

def reference(hidden_in, norm_gain, router_weight, expert_ids, gate_proj, up_proj, down_proj):
    blocks = N_EXPERT * N_HIDDEN
    normed = normalize(hidden_in, norm_gain)
    gates = gate_weights(normed, router_weight, expert_ids, EXPERTS)
    slot_place, slot_token, filled = jax.vmap(route_block)(expert_ids.reshape(blocks, TOK_DEV, TOP))
    buffers = jax.vmap(fill_block)(normed.reshape(blocks, TOK_DEV, D), slot_token, filled)
    per_expert = buffers.reshape(blocks, EXPERTS, CAP, D).transpose(1, 0, 2, 3).reshape(EXPERTS, blocks * CAP, D)
    outputs = lax.map(run_expert, (per_expert, gate_proj, up_proj, down_proj))
    returned = outputs.reshape(EXPERTS, blocks, CAP, D).transpose(1, 0, 2, 3).reshape(blocks, EXPERTS * CAP, D)
    picked = jax.vmap(pick_block)(returned, slot_place).reshape(TOKENS, TOP, D).astype(jnp.float32)
    mixture = lax.optimization_barrier(jnp.sum(gates[:, :, None] * picked, axis=1))
    return (hidden_in.astype(jnp.float32) + mixture).astype(jnp.bfloat16)
```

```python
import functools

import jax
import jax.numpy as jnp
from jax import lax
from jax.experimental import pallas as pl
from jax.experimental.pallas import tpu as pltpu
from jax.sharding import PartitionSpec as P


def normalize(hidden_in, norm_gain):
    values = hidden_in.astype(jnp.float32)
    factor = lax.rsqrt(jnp.mean(values * values, axis=-1, keepdims=True) + 1e-05)
    return (values * factor * norm_gain).astype(jnp.bfloat16)


def gate_weights(normed, router_weight, expert_ids, experts):
    logits = jnp.dot(normed, router_weight, preferred_element_type=jnp.float32)
    picks = expert_ids[:, :, None] == jnp.arange(experts, dtype=jnp.int32)[None, None, :]
    chosen = jnp.sum(jnp.where(picks, logits[:, None, :], 0.0), axis=-1)
    first = jax.nn.sigmoid(chosen[:, 0] - chosen[:, 1])
    return jnp.stack([first, 1.0 - first], axis=1)


def route_slots(block_ids, experts, capacity):
    flat_ids = block_ids.reshape(-1)
    count = jnp.arange(flat_ids.shape[0], dtype=jnp.int32)
    alike = jnp.logical_and(flat_ids[:, None] == flat_ids[None, :], count[None, :] < count[:, None])
    rank_in = jnp.sum(alike.astype(jnp.int32), axis=1)
    slot_place = flat_ids * capacity + rank_in
    owners = jnp.arange(flat_ids.shape[0], dtype=jnp.int32) // block_ids.shape[1]
    slot_token = jnp.zeros((experts * capacity,), jnp.int32).at[slot_place].set(owners)
    filled = jnp.zeros((experts * capacity,), jnp.bfloat16).at[slot_place].set(1.0)
    return (slot_place, slot_token, filled)


def routed_plan(hidden_in, norm_gain, router_weight, expert_ids, gate_proj, up_proj, down_proj):
    experts = lax.axis_size("expert")
    tok_rows = hidden_in.shape[0]
    width = hidden_in.shape[1]
    top_count = expert_ids.shape[1]
    capacity = 3 * tok_rows * top_count // (2 * experts)
    normed = normalize(hidden_in, norm_gain)
    gates = gate_weights(normed, router_weight, expert_ids, experts)
    slot_place, slot_token, filled = route_slots(expert_ids, experts, capacity)
    outgoing = (jnp.take(normed, slot_token, axis=0) * filled[:, None]).reshape(
        experts, capacity, width
    )
    arrived = lax.all_to_all(outgoing, "expert", split_axis=0, concat_axis=0, tiled=True)
    piece = lax.all_gather(arrived.reshape(experts * capacity, width), "hidden", axis=0, tiled=True)
    gate = jnp.dot(piece, gate_proj[0], preferred_element_type=jnp.float32)
    upper = jnp.dot(piece, up_proj[0], preferred_element_type=jnp.float32)
    inner = (jax.nn.silu(gate) * upper).astype(jnp.bfloat16)
    own_rows = lax.psum_scatter(
        jnp.dot(inner, down_proj[0], preferred_element_type=jnp.float32).astype(jnp.bfloat16),
        "hidden",
        scatter_dimension=0,
        tiled=True,
    )
    answers = own_rows.reshape(experts, capacity, width)
    returned = lax.all_to_all(answers, "expert", split_axis=0, concat_axis=0, tiled=True).reshape(
        experts * capacity, width
    )
    picked = (
        jnp.take(returned, slot_place, axis=0)
        .reshape(tok_rows, top_count, width)
        .astype(jnp.float32)
    )
    mixture = jnp.sum(gates[:, :, None] * picked, axis=1)
    return (hidden_in.astype(jnp.float32) + mixture).astype(jnp.bfloat16)


LANES = 128


def block_kernel(
    experts, nz,
    hid_ref, gain_ref, router_ref, ids_ref, wg_hbm, wu_hbm, wd_hbm,
    out_ref,
    wg, wu, wd, xs, act, part, from_sib, from_s, from_f, from_z,
    w_sems, ag_send, ag_recv, rs_send, rs_recv,
):
    rows, width = hid_ref.shape
    half = 4 * nz * rows
    hidden_units = wg.shape[1]

    def slot(s, plane, f, dz):
        return ((s * 2 + plane) * 2 + f) * nz + dz

    def at(number, count=1):
        return pl.ds(number * rows, count * rows)

    e = lax.axis_index("expert")
    h = lax.axis_index("hidden")
    core, x = e % 2, e // 2
    z, y = h // 2, h % 2
    e_other = (1 - x) * 2 + core
    h_other = z * 2 + (1 - y)
    first = (e * (1 - core) + e_other * core, h_other * (1 - core) + h * core)
    second = (e_other * (1 - core) + e * core, h * (1 - core) + h_other * core)
    sibling = (x * 2 + (1 - core), h)

    def z_peer(step):
        return (e, ((z + step) % nz) * 2 + y)

    loads = []
    for number, (source, target) in enumerate(((wg_hbm, wg), (wu_hbm, wu), (wd_hbm, wd))):
        loads.append(pltpu.make_async_copy(source.at[0], target, w_sems.at[number]))
        loads[-1].start()

    barrier = pltpu.get_barrier_semaphore()
    peers = [first, second, sibling] + [z_peer(step) for step in range(1, nz)]
    for peer in peers:
        pl.semaphore_signal(barrier, inc=1, device_id=peer, device_id_type=pl.DeviceIdType.MESH)

    values = hid_ref[...].astype(jnp.float32)
    factor = lax.rsqrt(jnp.mean(values * values, axis=-1, keepdims=True) + 1e-05)
    normed = (values * factor * gain_ref[...]).astype(jnp.bfloat16)
    xs[at(0), pl.ds(0, width)] = normed
    wide = normed.astype(jnp.float32)
    id0, id1 = ids_ref[:, 0:1], ids_ref[:, 1:2]
    l0 = jnp.zeros((rows, 1), jnp.float32)
    l1 = jnp.zeros((rows, 1), jnp.float32)
    for k in range(experts):
        logit = jnp.sum(wide * router_ref[k : k + 1, :].astype(jnp.float32), axis=-1, keepdims=True)
        l0 = l0 + jnp.where(id0 == k, logit, 0.0)
        l1 = l1 + jnp.where(id1 == k, logit, 0.0)
    g0 = 1.0 / (1.0 + jnp.exp(l1 - l0))
    g1 = 1.0 - g0
    lane = lax.broadcasted_iota(jnp.int32, (rows, LANES), 1)
    picked = lane % experts
    shares = jnp.where(picked == id0, g0, 0.0) + jnp.where(picked == id1, g1, 0.0)
    high = shares.astype(jnp.bfloat16)
    low = (shares - high.astype(jnp.float32)).astype(jnp.bfloat16)
    xs[at(0), pl.ds(width, LANES)] = jnp.where(
        lane < experts, high.astype(jnp.float32),
        jnp.where(lane < 2 * experts, low.astype(jnp.float32), 0.0),
    ).astype(jnp.bfloat16)

    pl.semaphore_wait(barrier, len(peers))

    sends = []

    def push(source_slot, target_slot, peer):
        copy = pltpu.make_async_remote_copy(
            src_ref=xs.at[at(source_slot)],
            dst_ref=xs.at[at(target_slot)],
            send_sem=ag_send.at[len(sends)],
            recv_sem=ag_recv.at[target_slot],
            device_id=peer,
            device_id_type=pl.DeviceIdType.MESH,
        )
        copy.start()
        sends.append(copy)

    def arrived(number):
        pltpu.make_async_copy(xs.at[at(number)], xs.at[at(number)], ag_recv.at[number]).wait()

    for step in range(1, nz):
        push(0, slot(0, 0, 0, nz - step), z_peer(step))
    push(0, slot(0, 0, 1, 0), first)
    push(0, slot(1, 0, 0, 0), second)
    push(0, slot(0, 1, 0, 0), sibling)
    for dz in range(1, nz):
        here = slot(0, 0, 0, dz)
        arrived(here)
        push(here, slot(0, 0, 1, dz), first)
        push(here, slot(1, 0, 0, dz), second)
        push(here, slot(0, 1, 0, dz), sibling)
    for dz in range(nz):
        here = slot(0, 0, 1, dz)
        arrived(here)
        push(here, slot(1, 0, 1, dz), second)
        push(here, slot(0, 1, 1, dz), sibling)
    for f in range(2):
        for dz in range(nz):
            here = slot(1, 0, f, dz)
            arrived(here)
            push(here, slot(1, 1, f, dz), sibling)
    for s in range(2):
        for f in range(2):
            for dz in range(nz):
                arrived(slot(s, 1, f, dz))

    loads[0].wait()
    loads[1].wait()

    def inner_half(start):
        lane_h = lax.broadcasted_iota(jnp.int32, (half, LANES), 1)
        tail = xs[pl.ds(start, half), pl.ds(width, LANES)].astype(jnp.float32)
        mine = jnp.logical_and(lane_h % experts == e, lane_h < 2 * experts)
        share = jnp.sum(jnp.where(mine, tail, 0.0), axis=-1, keepdims=True)

        @pl.loop(0, hidden_units // 256)
        def _(number):
            columns = pl.ds(pl.multiple_of(number * 256, 256), 256)
            block = xs[pl.ds(start, half), pl.ds(0, width)]
            gate = jnp.dot(block, wg[:, columns], preferred_element_type=jnp.float32)
            upper = jnp.dot(block, wu[:, columns], preferred_element_type=jnp.float32)
            inner = gate / (1.0 + jnp.exp(-gate)) * upper * share
            act[pl.ds(start, half), columns] = inner.astype(jnp.bfloat16)

    def down_half(start):
        @pl.loop(0, width // 512)
        def _(number):
            columns = pl.ds(pl.multiple_of(number * 512, 512), 512)
            part[pl.ds(start, half), columns] = jnp.dot(
                act[pl.ds(start, half), :], wd[:, columns], preferred_element_type=jnp.float32
            ).astype(jnp.bfloat16)

    inner_half(0)
    inner_half(half)
    loads[2].wait()

    returns = []

    def give(source, target, number, peer):
        copy = pltpu.make_async_remote_copy(
            src_ref=source,
            dst_ref=target,
            send_sem=rs_send.at[number],
            recv_sem=rs_recv.at[number],
            device_id=peer,
            device_id_type=pl.DeviceIdType.MESH,
        )
        copy.start()
        returns.append(copy)
        return copy

    def add(number, source):
        part[at(number), :] = (
            part[at(number), :].astype(jnp.float32) + source.astype(jnp.float32)
        ).astype(jnp.bfloat16)

    def to_sibling(s, f):
        number = s * 2 + f
        return give(
            part.at[at(slot(s, 1, f, 0), nz)], from_sib.at[at(number * nz, nz)], number, sibling
        )

    down_half(half)
    sib = {(1, f): to_sibling(1, f) for f in (1, 0)}
    down_half(0)
    for f in (1, 0):
        sib[0, f] = to_sibling(0, f)
    order = list(range(1, nz)) + [0]
    over_s, over_f, over_z = {}, {}, {}
    for f in (1, 0):
        sib[1, f].wait_recv()
        for dz in order:
            here = slot(1, 0, f, dz)
            add(here, from_sib[at((2 + f) * nz + dz), :])
            number = f * nz + dz
            over_s[f, dz] = give(part.at[at(here)], from_s.at[at(number)], 4 + number, second)
    sib[0, 1].wait_recv()
    for dz in order:
        here = slot(0, 0, 1, dz)
        add(here, from_sib[at(nz + dz), :])
        over_s[1, dz].wait_recv()
        add(here, from_s[at(nz + dz), :])
        over_f[dz] = give(part.at[at(here)], from_f.at[at(dz)], 4 + 2 * nz + dz, first)
    sib[0, 0].wait_recv()
    for dz in order:
        here = slot(0, 0, 0, dz)
        add(here, from_sib[at(dz), :])
        over_s[0, dz].wait_recv()
        add(here, from_s[at(dz), :])
        over_f[dz].wait_recv()
        if dz:
            add(here, from_f[at(dz), :])
            over_z[dz] = give(
                part.at[at(here)], from_z.at[at(nz - dz - 1)], 4 + 3 * nz + (nz - dz - 1), z_peer(dz)
            )
    total = part[at(slot(0, 0, 0, 0)), :].astype(jnp.float32) + from_f[at(0), :].astype(jnp.float32)
    for dz in range(1, nz):
        over_z[dz].wait_recv()
        total = total + from_z[at(nz - dz - 1), :].astype(jnp.float32)
    out_ref[...] = (hid_ref[...].astype(jnp.float32) + total).astype(out_ref.dtype)

    for copy in sends + returns:
        copy.wait_send()


def gathered_plan(hidden_in, norm_gain, router_weight, expert_ids, gate_proj, up_proj, down_proj):
    experts = lax.axis_size("expert")
    nz = lax.axis_size("hidden") // 2
    rows, width = hidden_in.shape
    units = gate_proj.shape[2]
    blocks = 8 * nz
    total = blocks * rows
    bf16 = jnp.bfloat16
    vmem = pl.BlockSpec(memory_space=pltpu.VMEM)
    hbm = pl.BlockSpec(memory_space=pl.ANY)
    return pl.pallas_call(
        functools.partial(block_kernel, experts, nz),
        out_shape=jax.ShapeDtypeStruct((rows, width), bf16),
        in_specs=[vmem] * 4 + [hbm] * 3,
        out_specs=vmem,
        scratch_shapes=[
            pltpu.VMEM((width, units), bf16),
            pltpu.VMEM((width, units), bf16),
            pltpu.VMEM((units, width), bf16),
            pltpu.VMEM((total, width + LANES), bf16),
            pltpu.VMEM((total, units), bf16),
            pltpu.VMEM((total, width), bf16),
            pltpu.VMEM((total // 2, width), bf16),
            pltpu.VMEM((total // 4, width), bf16),
            pltpu.VMEM((nz * rows, width), bf16),
            pltpu.VMEM(((nz - 1) * rows, width), bf16),
            pltpu.SemaphoreType.DMA((3,)),
            pltpu.SemaphoreType.DMA((blocks,)),
            pltpu.SemaphoreType.DMA((blocks,)),
            pltpu.SemaphoreType.DMA((4 + 4 * nz,)),
            pltpu.SemaphoreType.DMA((4 + 4 * nz,)),
        ],
        compiler_params=pltpu.CompilerParams(
            collective_id=0, has_side_effects=True, vmem_limit_bytes=62 * 1024 * 1024
        ),
        cost_estimate=pl.CostEstimate(
            flops=6 * total * width * units,
            bytes_accessed=6 * width * units,
            transcendentals=total * units,
        ),
    )(
        hidden_in, norm_gain.reshape(1, width), router_weight.T, expert_ids,
        gate_proj, up_proj, down_proj,
    )


def solution(mesh):
    experts, hidden = mesh.shape["expert"], mesh.shape["hidden"]

    def per_device(*arrays):
        tokens = experts * hidden * arrays[0].shape[0]
        width, units = arrays[4].shape[1:]
        held = 2 * width * (3 * units + 3 * tokens)
        square = experts == 4 and hidden % 2 == 0
        if square and held < 60 * 1024 * 1024:
            return gathered_plan(*arrays)
        return routed_plan(*arrays)

    placed = (
        P(("expert", "hidden"), None),
        P(),
        P(),
        P(("expert", "hidden"), None),
        P("expert", None, "hidden"),
        P("expert", None, "hidden"),
        P("expert", "hidden", None),
    )
    return jax.shard_map(
        per_device,
        mesh=mesh,
        in_specs=placed,
        out_specs=P(("expert", "hidden"), None),
        check_vma=False,
    )
```

```python
import functools

import jax
import jax.numpy as jnp
from jax import lax
from jax.experimental import pallas as pl
from jax.experimental.pallas import tpu as pltpu
from jax.sharding import PartitionSpec as P


def normalize(hidden_in, norm_gain):
    values = hidden_in.astype(jnp.float32)
    factor = lax.rsqrt(jnp.mean(values * values, axis=-1, keepdims=True) + 1e-05)
    return (values * factor * norm_gain).astype(jnp.bfloat16)


def gate_weights(normed, router_weight, expert_ids, experts):
    logits = jnp.dot(normed, router_weight, preferred_element_type=jnp.float32)
    picks = expert_ids[:, :, None] == jnp.arange(experts, dtype=jnp.int32)[None, None, :]
    chosen = jnp.sum(jnp.where(picks, logits[:, None, :], 0.0), axis=-1)
    first = jax.nn.sigmoid(chosen[:, 0] - chosen[:, 1])
    return jnp.stack([first, 1.0 - first], axis=1)


def route_slots(block_ids, experts, capacity):
    flat_ids = block_ids.reshape(-1)
    count = jnp.arange(flat_ids.shape[0], dtype=jnp.int32)
    alike = jnp.logical_and(flat_ids[:, None] == flat_ids[None, :], count[None, :] < count[:, None])
    rank_in = jnp.sum(alike.astype(jnp.int32), axis=1)
    slot_place = flat_ids * capacity + rank_in
    owners = jnp.arange(flat_ids.shape[0], dtype=jnp.int32) // block_ids.shape[1]
    slot_token = jnp.zeros((experts * capacity,), jnp.int32).at[slot_place].set(owners)
    filled = jnp.zeros((experts * capacity,), jnp.bfloat16).at[slot_place].set(1.0)
    return (slot_place, slot_token, filled)


def routed_plan(hidden_in, norm_gain, router_weight, expert_ids, gate_proj, up_proj, down_proj):
    experts = lax.axis_size("expert")
    tok_rows = hidden_in.shape[0]
    width = hidden_in.shape[1]
    top_count = expert_ids.shape[1]
    capacity = 3 * tok_rows * top_count // (2 * experts)
    normed = normalize(hidden_in, norm_gain)
    gates = gate_weights(normed, router_weight, expert_ids, experts)
    slot_place, slot_token, filled = route_slots(expert_ids, experts, capacity)
    outgoing = (jnp.take(normed, slot_token, axis=0) * filled[:, None]).reshape(
        experts, capacity, width
    )
    arrived = lax.all_to_all(outgoing, "expert", split_axis=0, concat_axis=0, tiled=True)
    piece = lax.all_gather(arrived.reshape(experts * capacity, width), "hidden", axis=0, tiled=True)
    gate = jnp.dot(piece, gate_proj[0], preferred_element_type=jnp.float32)
    upper = jnp.dot(piece, up_proj[0], preferred_element_type=jnp.float32)
    inner = (jax.nn.silu(gate) * upper).astype(jnp.bfloat16)
    own_rows = lax.psum_scatter(
        jnp.dot(inner, down_proj[0], preferred_element_type=jnp.float32).astype(jnp.bfloat16),
        "hidden",
        scatter_dimension=0,
        tiled=True,
    )
    answers = own_rows.reshape(experts, capacity, width)
    returned = lax.all_to_all(answers, "expert", split_axis=0, concat_axis=0, tiled=True).reshape(
        experts * capacity, width
    )
    picked = (
        jnp.take(returned, slot_place, axis=0)
        .reshape(tok_rows, top_count, width)
        .astype(jnp.float32)
    )
    mixture = jnp.sum(gates[:, :, None] * picked, axis=1)
    return (hidden_in.astype(jnp.float32) + mixture).astype(jnp.bfloat16)


LANES = 128


def block_kernel(
    experts, nz,
    hid_ref, gain_ref, router_ref, ids_ref, wg_hbm, wu_hbm, wd_hbm,
    out_ref,
    wg, wu, wd, xs, act, part, from_sib, from_s, from_f, from_z,
    w_sems, ag_send, ag_recv, rs_send, rs_recv,
):
    rows, width = hid_ref.shape
    half = 4 * nz * rows
    hidden_units = wg.shape[1]

    def slot(s, plane, f, dz):
        return ((s * 2 + plane) * 2 + f) * nz + dz

    def at(number, count=1):
        return pl.ds(number * rows, count * rows)

    e = lax.axis_index("expert")
    h = lax.axis_index("hidden")
    core, x = e % 2, e // 2
    z, y = h // 2, h % 2
    e_other = (1 - x) * 2 + core
    h_other = z * 2 + (1 - y)
    first = (e * (1 - core) + e_other * core, h_other * (1 - core) + h * core)
    second = (e_other * (1 - core) + e * core, h * (1 - core) + h_other * core)
    sibling = (x * 2 + (1 - core), h)

    def z_peer(step):
        return (e, ((z + step) % nz) * 2 + y)

    loads = []
    for number, (source, target) in enumerate(((wg_hbm, wg), (wu_hbm, wu), (wd_hbm, wd))):
        loads.append(pltpu.make_async_copy(source.at[0], target, w_sems.at[number]))
        loads[-1].start()

    barrier = pltpu.get_barrier_semaphore()
    peers = [first, second, sibling] + [z_peer(step) for step in range(1, nz)]
    for peer in peers:
        pl.semaphore_signal(barrier, inc=1, device_id=peer, device_id_type=pl.DeviceIdType.MESH)

    values = hid_ref[...].astype(jnp.float32)
    factor = lax.rsqrt(jnp.mean(values * values, axis=-1, keepdims=True) + 1e-05)
    normed = (values * factor * gain_ref[...]).astype(jnp.bfloat16)
    xs[at(0), pl.ds(0, width)] = normed
    wide = normed.astype(jnp.float32)
    id0, id1 = ids_ref[:, 0:1], ids_ref[:, 1:2]
    l0 = jnp.zeros((rows, 1), jnp.float32)
    l1 = jnp.zeros((rows, 1), jnp.float32)
    for k in range(experts):
        logit = jnp.sum(wide * router_ref[k : k + 1, :].astype(jnp.float32), axis=-1, keepdims=True)
        l0 = l0 + jnp.where(id0 == k, logit, 0.0)
        l1 = l1 + jnp.where(id1 == k, logit, 0.0)
    g0 = 1.0 / (1.0 + jnp.exp(l1 - l0))
    g1 = 1.0 - g0
    lane = lax.broadcasted_iota(jnp.int32, (rows, LANES), 1)
    picked = lane % experts
    shares = jnp.where(picked == id0, g0, 0.0) + jnp.where(picked == id1, g1, 0.0)
    high = shares.astype(jnp.bfloat16)
    low = (shares - high.astype(jnp.float32)).astype(jnp.bfloat16)
    xs[at(0), pl.ds(width, LANES)] = jnp.where(
        lane < experts, high.astype(jnp.float32),
        jnp.where(lane < 2 * experts, low.astype(jnp.float32), 0.0),
    ).astype(jnp.bfloat16)

    pl.semaphore_wait(barrier, len(peers))

    sends = []

    def push(source_slot, target_slot, peer):
        copy = pltpu.make_async_remote_copy(
            src_ref=xs.at[at(source_slot)],
            dst_ref=xs.at[at(target_slot)],
            send_sem=ag_send.at[len(sends)],
            recv_sem=ag_recv.at[target_slot],
            device_id=peer,
            device_id_type=pl.DeviceIdType.MESH,
        )
        copy.start()
        sends.append(copy)

    def arrived(number):
        pltpu.make_async_copy(xs.at[at(number)], xs.at[at(number)], ag_recv.at[number]).wait()

    near = sorted(range(1, nz), key=lambda step: min(step, nz - step))
    for step in near:
        push(0, slot(0, 0, 0, nz - step), z_peer(step))
    push(0, slot(0, 0, 1, 0), first)
    push(0, slot(1, 0, 0, 0), second)
    push(0, slot(0, 1, 0, 0), sibling)
    for dz in near:
        here = slot(0, 0, 0, dz)
        arrived(here)
        push(here, slot(0, 0, 1, dz), first)
        push(here, slot(1, 0, 0, dz), second)
        push(here, slot(0, 1, 0, dz), sibling)
    for dz in [0] + near:
        here = slot(0, 0, 1, dz)
        arrived(here)
        push(here, slot(1, 0, 1, dz), second)
        push(here, slot(0, 1, 1, dz), sibling)

    def inner_half(start):
        lane_h = lax.broadcasted_iota(jnp.int32, (half, LANES), 1)
        tail = xs[pl.ds(start, half), pl.ds(width, LANES)].astype(jnp.float32)
        mine = jnp.logical_and(lane_h % experts == e, lane_h < 2 * experts)
        share = jnp.sum(jnp.where(mine, tail, 0.0), axis=-1, keepdims=True)

        @pl.loop(0, hidden_units // 256)
        def _(number):
            columns = pl.ds(pl.multiple_of(number * 256, 256), 256)
            block = xs[pl.ds(start, half), pl.ds(0, width)]
            gate = jnp.dot(block, wg[:, columns], preferred_element_type=jnp.float32)
            upper = jnp.dot(block, wu[:, columns], preferred_element_type=jnp.float32)
            inner = gate / (1.0 + jnp.exp(-gate)) * upper * share
            act[pl.ds(start, half), columns] = inner.astype(jnp.bfloat16)

    def down_half(start):
        @pl.loop(0, width // 512)
        def _(number):
            columns = pl.ds(pl.multiple_of(number * 512, 512), 512)
            part[pl.ds(start, half), columns] = jnp.dot(
                act[pl.ds(start, half), :], wd[:, columns], preferred_element_type=jnp.float32
            ).astype(jnp.bfloat16)

    returns = []

    def give(source, target, number, peer):
        copy = pltpu.make_async_remote_copy(
            src_ref=source,
            dst_ref=target,
            send_sem=rs_send.at[number],
            recv_sem=rs_recv.at[number],
            device_id=peer,
            device_id_type=pl.DeviceIdType.MESH,
        )
        copy.start()
        returns.append(copy)
        return copy

    def add(number, source):
        part[at(number), :] = (
            part[at(number), :].astype(jnp.float32) + source.astype(jnp.float32)
        ).astype(jnp.bfloat16)

    def to_sibling(s, f):
        number = s * 2 + f
        return give(
            part.at[at(slot(s, 1, f, 0), nz)], from_sib.at[at(number * nz, nz)], number, sibling
        )

    for f in range(2):
        for dz in [0] + near:
            arrived(slot(0, 1, f, dz))
    loads[0].wait()
    loads[1].wait()
    inner_half(0)
    loads[2].wait()
    down_half(0)
    sib = {(0, f): to_sibling(0, f) for f in (1, 0)}
    for f in range(2):
        for dz in [0] + near:
            here = slot(1, 0, f, dz)
            arrived(here)
            push(here, slot(1, 1, f, dz), sibling)
    for f in range(2):
        for dz in [0] + near:
            arrived(slot(1, 1, f, dz))
    inner_half(half)
    down_half(half)
    for f in (1, 0):
        sib[1, f] = to_sibling(1, f)
    order = near[::-1] + [0]
    over_s, over_f, over_z = {}, {}, {}
    for f in (1, 0):
        sib[1, f].wait_recv()
        for dz in order:
            here = slot(1, 0, f, dz)
            add(here, from_sib[at((2 + f) * nz + dz), :])
            number = f * nz + dz
            over_s[f, dz] = give(part.at[at(here)], from_s.at[at(number)], 4 + number, second)
    for f in (1, 0):
        sib[0, f].wait_recv()
        for dz in order:
            add(slot(0, 0, f, dz), from_sib[at(f * nz + dz), :])
    for dz in order:
        here = slot(0, 0, 1, dz)
        over_s[1, dz].wait_recv()
        add(here, from_s[at(nz + dz), :])
        over_f[dz] = give(part.at[at(here)], from_f.at[at(dz)], 4 + 2 * nz + dz, first)
    for dz in order:
        here = slot(0, 0, 0, dz)
        over_s[0, dz].wait_recv()
        add(here, from_s[at(dz), :])
        over_f[dz].wait_recv()
        if dz:
            add(here, from_f[at(dz), :])
            over_z[dz] = give(
                part.at[at(here)], from_z.at[at(nz - dz - 1)], 4 + 3 * nz + (nz - dz - 1), z_peer(dz)
            )
    total = part[at(slot(0, 0, 0, 0)), :].astype(jnp.float32) + from_f[at(0), :].astype(jnp.float32)
    for dz in range(1, nz):
        over_z[dz].wait_recv()
        total = total + from_z[at(nz - dz - 1), :].astype(jnp.float32)
    out_ref[...] = (hid_ref[...].astype(jnp.float32) + total).astype(out_ref.dtype)

    for copy in sends + returns:
        copy.wait_send()


def gathered_plan(hidden_in, norm_gain, router_weight, expert_ids, gate_proj, up_proj, down_proj):
    experts = lax.axis_size("expert")
    nz = lax.axis_size("hidden") // 2
    rows, width = hidden_in.shape
    units = gate_proj.shape[2]
    blocks = 8 * nz
    total = blocks * rows
    bf16 = jnp.bfloat16
    vmem = pl.BlockSpec(memory_space=pltpu.VMEM)
    hbm = pl.BlockSpec(memory_space=pl.ANY)
    return pl.pallas_call(
        functools.partial(block_kernel, experts, nz),
        out_shape=jax.ShapeDtypeStruct((rows, width), bf16),
        in_specs=[vmem] * 4 + [hbm] * 3,
        out_specs=vmem,
        scratch_shapes=[
            pltpu.VMEM((width, units), bf16),
            pltpu.VMEM((width, units), bf16),
            pltpu.VMEM((units, width), bf16),
            pltpu.VMEM((total, width + LANES), bf16),
            pltpu.VMEM((total, units), bf16),
            pltpu.VMEM((total, width), bf16),
            pltpu.VMEM((total // 2, width), bf16),
            pltpu.VMEM((total // 4, width), bf16),
            pltpu.VMEM((nz * rows, width), bf16),
            pltpu.VMEM(((nz - 1) * rows, width), bf16),
            pltpu.SemaphoreType.DMA((3,)),
            pltpu.SemaphoreType.DMA((blocks,)),
            pltpu.SemaphoreType.DMA((blocks,)),
            pltpu.SemaphoreType.DMA((4 + 4 * nz,)),
            pltpu.SemaphoreType.DMA((4 + 4 * nz,)),
        ],
        compiler_params=pltpu.CompilerParams(
            collective_id=0, has_side_effects=True, vmem_limit_bytes=62 * 1024 * 1024
        ),
        cost_estimate=pl.CostEstimate(
            flops=6 * total * width * units,
            bytes_accessed=6 * width * units,
            transcendentals=total * units,
        ),
    )(
        hidden_in, norm_gain.reshape(1, width), router_weight.T, expert_ids,
        gate_proj, up_proj, down_proj,
    )


def solution(mesh):
    experts, hidden = mesh.shape["expert"], mesh.shape["hidden"]

    def per_device(*arrays):
        tokens = experts * hidden * arrays[0].shape[0]
        width, units = arrays[4].shape[1:]
        held = 2 * width * (3 * units + 3 * tokens)
        square = experts == 4 and hidden % 2 == 0
        if square and held < 60 * 1024 * 1024:
            return gathered_plan(*arrays)
        return routed_plan(*arrays)

    placed = (
        P(("expert", "hidden"), None),
        P(),
        P(),
        P(("expert", "hidden"), None),
        P("expert", None, "hidden"),
        P("expert", None, "hidden"),
        P("expert", "hidden", None),
    )
    return jax.shard_map(
        per_device,
        mesh=mesh,
        in_specs=placed,
        out_specs=P(("expert", "hidden"), None),
        check_vma=False,
    )
```

```python
import functools

import jax
import jax.numpy as jnp
from jax import lax
from jax.experimental import pallas as pl
from jax.experimental.pallas import tpu as pltpu
from jax.sharding import PartitionSpec as P


def normalize(hidden_in, norm_gain):
    values = hidden_in.astype(jnp.float32)
    factor = lax.rsqrt(jnp.mean(values * values, axis=-1, keepdims=True) + 1e-05)
    return (values * factor * norm_gain).astype(jnp.bfloat16)


def gate_weights(normed, router_weight, expert_ids, experts):
    logits = jnp.dot(normed, router_weight, preferred_element_type=jnp.float32)
    picks = expert_ids[:, :, None] == jnp.arange(experts, dtype=jnp.int32)[None, None, :]
    chosen = jnp.sum(jnp.where(picks, logits[:, None, :], 0.0), axis=-1)
    first = jax.nn.sigmoid(chosen[:, 0] - chosen[:, 1])
    return jnp.stack([first, 1.0 - first], axis=1)


def route_slots(block_ids, experts, capacity):
    flat_ids = block_ids.reshape(-1)
    count = jnp.arange(flat_ids.shape[0], dtype=jnp.int32)
    alike = jnp.logical_and(flat_ids[:, None] == flat_ids[None, :], count[None, :] < count[:, None])
    rank_in = jnp.sum(alike.astype(jnp.int32), axis=1)
    slot_place = flat_ids * capacity + rank_in
    owners = jnp.arange(flat_ids.shape[0], dtype=jnp.int32) // block_ids.shape[1]
    slot_token = jnp.zeros((experts * capacity,), jnp.int32).at[slot_place].set(owners)
    filled = jnp.zeros((experts * capacity,), jnp.bfloat16).at[slot_place].set(1.0)
    return (slot_place, slot_token, filled)


def routed_plan(hidden_in, norm_gain, router_weight, expert_ids, gate_proj, up_proj, down_proj):
    experts = lax.axis_size("expert")
    tok_rows = hidden_in.shape[0]
    width = hidden_in.shape[1]
    top_count = expert_ids.shape[1]
    capacity = 3 * tok_rows * top_count // (2 * experts)
    normed = normalize(hidden_in, norm_gain)
    gates = gate_weights(normed, router_weight, expert_ids, experts)
    slot_place, slot_token, filled = route_slots(expert_ids, experts, capacity)
    outgoing = (jnp.take(normed, slot_token, axis=0) * filled[:, None]).reshape(
        experts, capacity, width
    )
    arrived = lax.all_to_all(outgoing, "expert", split_axis=0, concat_axis=0, tiled=True)
    piece = lax.all_gather(arrived.reshape(experts * capacity, width), "hidden", axis=0, tiled=True)
    gate = jnp.dot(piece, gate_proj[0], preferred_element_type=jnp.float32)
    upper = jnp.dot(piece, up_proj[0], preferred_element_type=jnp.float32)
    inner = (jax.nn.silu(gate) * upper).astype(jnp.bfloat16)
    own_rows = lax.psum_scatter(
        jnp.dot(inner, down_proj[0], preferred_element_type=jnp.float32).astype(jnp.bfloat16),
        "hidden",
        scatter_dimension=0,
        tiled=True,
    )
    answers = own_rows.reshape(experts, capacity, width)
    returned = lax.all_to_all(answers, "expert", split_axis=0, concat_axis=0, tiled=True).reshape(
        experts * capacity, width
    )
    picked = (
        jnp.take(returned, slot_place, axis=0)
        .reshape(tok_rows, top_count, width)
        .astype(jnp.float32)
    )
    mixture = jnp.sum(gates[:, :, None] * picked, axis=1)
    return (hidden_in.astype(jnp.float32) + mixture).astype(jnp.bfloat16)


LANES = 128


def block_kernel(
    experts, nz,
    hid_ref, gain_ref, router_ref, ids_ref, wg_hbm, wu_hbm, wd_hbm,
    out_ref,
    wg, wu, wd, xs, act, part, from_sib, from_one, from_two, from_z,
    w_sems, ag_send, ag_recv, rs_send, rs_recv,
):
    rows, width = hid_ref.shape
    half = 4 * nz * rows
    hidden_units = wg.shape[1]

    def slot(s, plane, f, dz):
        return ((s * 2 + plane) * 2 + f) * nz + dz

    def at(number, count=1):
        return pl.ds(number * rows, count * rows)

    e = lax.axis_index("expert")
    h = lax.axis_index("hidden")
    core, x = e % 2, e // 2
    z, y = h // 2, h % 2
    e_other = (1 - x) * 2 + core
    h_other = z * 2 + (1 - y)
    first = (e * (1 - core) + e_other * core, h_other * (1 - core) + h * core)
    second = (e_other * (1 - core) + e * core, h * (1 - core) + h_other * core)
    sibling = (x * 2 + (1 - core), h)

    def z_peer(step):
        return (e, ((z + step) % nz) * 2 + y)

    loads = []
    for number, (source, target) in enumerate(((wg_hbm, wg), (wu_hbm, wu), (wd_hbm, wd))):
        loads.append(pltpu.make_async_copy(source.at[0], target, w_sems.at[number]))
        loads[-1].start()

    barrier = pltpu.get_barrier_semaphore()
    peers = [first, second, sibling] + [z_peer(step) for step in range(1, nz)]
    for peer in peers:
        pl.semaphore_signal(barrier, inc=1, device_id=peer, device_id_type=pl.DeviceIdType.MESH)

    values = hid_ref[...].astype(jnp.float32)
    factor = lax.rsqrt(jnp.mean(values * values, axis=-1, keepdims=True) + 1e-05)
    normed = (values * factor * gain_ref[...]).astype(jnp.bfloat16)
    xs[at(0), pl.ds(0, width)] = normed
    wide = normed.astype(jnp.float32)
    id0, id1 = ids_ref[:, 0:1], ids_ref[:, 1:2]
    l0 = jnp.zeros((rows, 1), jnp.float32)
    l1 = jnp.zeros((rows, 1), jnp.float32)
    for k in range(experts):
        logit = jnp.sum(wide * router_ref[k : k + 1, :].astype(jnp.float32), axis=-1, keepdims=True)
        l0 = l0 + jnp.where(id0 == k, logit, 0.0)
        l1 = l1 + jnp.where(id1 == k, logit, 0.0)
    g0 = 1.0 / (1.0 + jnp.exp(l1 - l0))
    g1 = 1.0 - g0
    lane = lax.broadcasted_iota(jnp.int32, (rows, LANES), 1)
    picked = lane % experts
    shares = jnp.where(picked == id0, g0, 0.0) + jnp.where(picked == id1, g1, 0.0)
    high = shares.astype(jnp.bfloat16)
    low = (shares - high.astype(jnp.float32)).astype(jnp.bfloat16)
    xs[at(0), pl.ds(width, LANES)] = jnp.where(
        lane < experts, high.astype(jnp.float32),
        jnp.where(lane < 2 * experts, low.astype(jnp.float32), 0.0),
    ).astype(jnp.bfloat16)

    pl.semaphore_wait(barrier, len(peers))

    sends = []

    def push(source_slot, target_slot, peer):
        copy = pltpu.make_async_remote_copy(
            src_ref=xs.at[at(source_slot)],
            dst_ref=xs.at[at(target_slot)],
            send_sem=ag_send.at[len(sends)],
            recv_sem=ag_recv.at[target_slot],
            device_id=peer,
            device_id_type=pl.DeviceIdType.MESH,
        )
        copy.start()
        sends.append(copy)

    def arrived(number):
        pltpu.make_async_copy(xs.at[at(number)], xs.at[at(number)], ag_recv.at[number]).wait()

    near = sorted(range(1, nz), key=lambda step: min(step, nz - step))
    for step in near:
        push(0, slot(0, 0, 0, nz - step), z_peer(step))
    push(0, slot(0, 0, 1, 0), first)
    push(0, slot(1, 0, 0, 0), second)
    push(0, slot(0, 1, 0, 0), sibling)
    for dz in near:
        here = slot(0, 0, 0, dz)
        arrived(here)
        push(here, slot(0, 0, 1, dz), first)
        push(here, slot(1, 0, 0, dz), second)
        push(here, slot(0, 1, 0, dz), sibling)
    for dz in [0] + near:
        here = slot(0, 0, 1, dz)
        arrived(here)
        push(here, slot(1, 0, 1, dz), second)
        push(here, slot(0, 1, 1, dz), sibling)

    def inner_half(start):
        lane_h = lax.broadcasted_iota(jnp.int32, (half, LANES), 1)
        tail = xs[pl.ds(start, half), pl.ds(width, LANES)].astype(jnp.float32)
        mine = jnp.logical_and(lane_h % experts == e, lane_h < 2 * experts)
        share = jnp.sum(jnp.where(mine, tail, 0.0), axis=-1, keepdims=True)

        @pl.loop(0, hidden_units // 256)
        def _(number):
            columns = pl.ds(pl.multiple_of(number * 256, 256), 256)
            block = xs[pl.ds(start, half), pl.ds(0, width)]
            gate = jnp.dot(block, wg[:, columns], preferred_element_type=jnp.float32)
            upper = jnp.dot(block, wu[:, columns], preferred_element_type=jnp.float32)
            inner = gate / (1.0 + jnp.exp(-gate)) * upper * share
            act[pl.ds(start, half), columns] = inner.astype(jnp.bfloat16)

    def down_half(start):
        @pl.loop(0, width // 512)
        def _(number):
            columns = pl.ds(pl.multiple_of(number * 512, 512), 512)
            part[pl.ds(start, half), columns] = jnp.dot(
                act[pl.ds(start, half), :], wd[:, columns], preferred_element_type=jnp.float32
            ).astype(jnp.bfloat16)

    returns = []

    def give(source, target, number, peer):
        copy = pltpu.make_async_remote_copy(
            src_ref=source,
            dst_ref=target,
            send_sem=rs_send.at[number],
            recv_sem=rs_recv.at[number],
            device_id=peer,
            device_id_type=pl.DeviceIdType.MESH,
        )
        copy.start()
        returns.append(copy)
        return copy

    def add(number, source):
        part[at(number), :] = (
            part[at(number), :].astype(jnp.float32) + source.astype(jnp.float32)
        ).astype(jnp.bfloat16)

    def to_sibling(s, f):
        number = s * 2 + f
        return give(
            part.at[at(slot(s, 1, f, 0), nz)], from_sib.at[at(number * nz, nz)], number, sibling
        )

    for f in range(2):
        for dz in [0] + near:
            arrived(slot(0, 1, f, dz))
    loads[0].wait()
    loads[1].wait()
    inner_half(0)
    loads[2].wait()
    down_half(0)
    sib = {(0, f): to_sibling(0, f) for f in (1, 0)}
    for f in range(2):
        for dz in [0] + near:
            here = slot(1, 0, f, dz)
            arrived(here)
            push(here, slot(1, 1, f, dz), sibling)
    order = near[::-1] + [0]
    over_one, over_two, over_z = {}, {}, {}

    def reduce_first(s):
        sib[s, 1].wait_recv()
        for dz in order:
            here = slot(s, 0, 1, dz)
            add(here, from_sib[at((2 * s + 1) * nz + dz), :])
            number = s * nz + dz
            over_one[s, dz] = give(part.at[at(here)], from_one.at[at(number)], 4 + number, first)

    def reduce_own(s):
        sib[s, 0].wait_recv()
        for dz in order:
            add(slot(s, 0, 0, dz), from_sib[at(2 * s * nz + dz), :])

    reduce_first(0)
    for f in range(2):
        for dz in [0] + near:
            arrived(slot(1, 1, f, dz))
    inner_half(half)
    down_half(half)
    for f in (1, 0):
        sib[1, f] = to_sibling(1, f)
    reduce_first(1)
    reduce_own(1)
    reduce_own(0)
    for dz in order:
        over_one[0, dz].wait_recv()
        add(slot(0, 0, 0, dz), from_one[at(dz), :])
    for dz in order:
        here = slot(1, 0, 0, dz)
        over_one[1, dz].wait_recv()
        add(here, from_one[at(nz + dz), :])
        over_two[dz] = give(part.at[at(here)], from_two.at[at(dz)], 4 + 2 * nz + dz, second)
    for dz in order:
        here = slot(0, 0, 0, dz)
        over_two[dz].wait_recv()
        if dz:
            add(here, from_two[at(dz), :])
            over_z[dz] = give(
                part.at[at(here)], from_z.at[at(nz - dz - 1)], 4 + 3 * nz + (nz - dz - 1), z_peer(dz)
            )
    total = part[at(slot(0, 0, 0, 0)), :].astype(jnp.float32) + from_two[at(0), :].astype(jnp.float32)
    for dz in range(1, nz):
        over_z[dz].wait_recv()
        total = total + from_z[at(nz - dz - 1), :].astype(jnp.float32)
    out_ref[...] = (hid_ref[...].astype(jnp.float32) + total).astype(out_ref.dtype)

    for copy in sends + returns:
        copy.wait_send()


def gathered_plan(hidden_in, norm_gain, router_weight, expert_ids, gate_proj, up_proj, down_proj):
    experts = lax.axis_size("expert")
    nz = lax.axis_size("hidden") // 2
    rows, width = hidden_in.shape
    units = gate_proj.shape[2]
    blocks = 8 * nz
    total = blocks * rows
    bf16 = jnp.bfloat16
    vmem = pl.BlockSpec(memory_space=pltpu.VMEM)
    hbm = pl.BlockSpec(memory_space=pl.ANY)
    return pl.pallas_call(
        functools.partial(block_kernel, experts, nz),
        out_shape=jax.ShapeDtypeStruct((rows, width), bf16),
        in_specs=[vmem] * 4 + [hbm] * 3,
        out_specs=vmem,
        scratch_shapes=[
            pltpu.VMEM((width, units), bf16),
            pltpu.VMEM((width, units), bf16),
            pltpu.VMEM((units, width), bf16),
            pltpu.VMEM((total, width + LANES), bf16),
            pltpu.VMEM((total, units), bf16),
            pltpu.VMEM((total, width), bf16),
            pltpu.VMEM((total // 2, width), bf16),
            pltpu.VMEM((total // 4, width), bf16),
            pltpu.VMEM((nz * rows, width), bf16),
            pltpu.VMEM(((nz - 1) * rows, width), bf16),
            pltpu.SemaphoreType.DMA((3,)),
            pltpu.SemaphoreType.DMA((blocks,)),
            pltpu.SemaphoreType.DMA((blocks,)),
            pltpu.SemaphoreType.DMA((4 + 4 * nz,)),
            pltpu.SemaphoreType.DMA((4 + 4 * nz,)),
        ],
        compiler_params=pltpu.CompilerParams(
            collective_id=0, has_side_effects=True, vmem_limit_bytes=62 * 1024 * 1024
        ),
        cost_estimate=pl.CostEstimate(
            flops=6 * total * width * units,
            bytes_accessed=6 * width * units,
            transcendentals=total * units,
        ),
    )(
        hidden_in, norm_gain.reshape(1, width), router_weight.T, expert_ids,
        gate_proj, up_proj, down_proj,
    )


def solution(mesh):
    experts, hidden = mesh.shape["expert"], mesh.shape["hidden"]

    def per_device(*arrays):
        tokens = experts * hidden * arrays[0].shape[0]
        width, units = arrays[4].shape[1:]
        held = 2 * width * (3 * units + 3 * tokens)
        square = experts == 4 and hidden % 2 == 0
        if square and held < 60 * 1024 * 1024:
            return gathered_plan(*arrays)
        return routed_plan(*arrays)

    placed = (
        P(("expert", "hidden"), None),
        P(),
        P(),
        P(("expert", "hidden"), None),
        P("expert", None, "hidden"),
        P("expert", None, "hidden"),
        P("expert", "hidden", None),
    )
    return jax.shard_map(
        per_device,
        mesh=mesh,
        in_specs=placed,
        out_specs=P(("expert", "hidden"), None),
        check_vma=False,
    )
```
